256 devices in a mesh: rows: 64 (over x, z, core), group: 4 (over y).
Axes of the slice: x: 4, y: 4, z: 8, core: 2. Of those that a mesh axis runs over, the one named last changes fastest.
Arguments:
- scores: bfloat16 [262144, 1024], P(('rows', 'group'))
- worker_ids: int32 [262144], P(('rows', 'group')), may hold values from 0 to 65535, as said below
- firm_ids: int32 [262144], P(('rows', 'group')), may hold values from 0 to 32767, as said below
Outputs:
- meat: float32 [1024, 1024], P('rows', 'group')
The draws below stay inside these ranges and needn't reach their ends.
Inputs may be any that keep to these rules, and one draw needn't show every extreme that they name: `worker_ids`: among the rows of one device, at most 8 have worker ids of one residue mod 256, and on every device some residue has exactly 8. `firm_ids`: every worker names at most two firms. Among the rows of one device, at most 8 have firm ids of one residue mod 256, and on every device some residue has exactly 8. For any residues a and b mod 256, at most 2 distinct worker-firm pairs have a worker of residue a and a firm of residue b, and some a and b have exactly 2.
All inputs are finite; a program needn't handle non-finite values.
Results may differ from the reference program's by a relative error of at most 0.0035.
Values may be sent and summed in bfloat16 or wider, within the bound.
No kernel may reach another device: no remote copies, remote signals or barrier semaphores. Data moves between devices by JAX's collectives and lax.ppermute only.
A program may use at most 64 MiB of HBM per device.

```python
import jax
import jax.numpy as jnp
from jax import lax

K = 1024
ROWS_DEV = 1024
CW_DEV = 256
CF_DEV = 128
WORKERS = 65536
FIRMS = 32768
TOTAL = 262144
N_ROWS = 64
N_GROUP = 4


def balanced_homes(key, classes):
    capacity = 2 * ROWS_DEV // classes
    half_cap = capacity // 2
    subkeys = jax.random.split(key, 3)
    offsets = jax.random.randint(subkeys[0], (classes, classes), 0, half_cap + 1)
    forced = jax.random.randint(subkeys[1], (classes, 1), 0, classes)
    columns = jnp.arange(classes, dtype=jnp.int32)[None, :]
    offsets = jnp.where(columns == forced, half_cap, offsets)
    offsets = jnp.where(columns == (forced + 1) % classes, 0, offsets)
    counts = half_cap + offsets - jnp.roll(offsets, -1, axis=1)
    bounds = jnp.cumsum(counts, axis=1)
    position = jnp.arange(ROWS_DEV, dtype=jnp.int32)

    def locate(edges):
        return jnp.searchsorted(edges, position, side='right')
    sorted_home = jax.vmap(locate)(bounds).astype(jnp.int32)
    return jax.random.permutation(subkeys[2], sorted_home, axis=1, independent=True)


def cluster_ids(key):
    classes = N_ROWS * N_GROUP
    spread = CW_DEV // classes
    subkeys = jax.random.split(key, 7)
    worker_home = balanced_homes(subkeys[0], classes)
    firm_home = balanced_homes(subkeys[1], classes)
    ordinal = jax.random.randint(subkeys[2], (classes, ROWS_DEV), 0, 2)
    block = jax.random.randint(subkeys[3], (classes, ROWS_DEV), 0, spread)
    second_offset = jax.random.randint(subkeys[4], (classes, spread), 1, classes)
    distance = (firm_home - worker_home) % classes
    base = jnp.where(ordinal == 1, (distance - second_offset[worker_home, block]) % classes, distance)
    unmixed = base + classes * block
    order = jnp.tile(jnp.arange(CW_DEV, dtype=jnp.int32)[None, :], (classes, 1))
    shuffled = jax.random.permutation(subkeys[5], order, axis=1, independent=True)
    worker_local = shuffled[worker_home, unmixed]
    worker = worker_home + classes * worker_local
    levels = jax.random.randint(subkeys[6], (2, WORKERS), 0, 4096)
    firm_table = jnp.minimum(levels * levels // (16777216 // CF_DEV), CF_DEV - 1)
    firm_local = firm_table[ordinal, worker]
    firm_id = firm_home + classes * firm_local
    return (worker.reshape(-1).astype(jnp.int32), firm_id.reshape(-1).astype(jnp.int32), ordinal.reshape(-1).astype(jnp.int32))


def draw_worker_ids(key, part):
    return cluster_ids(key)[0]


def draw_firm_ids(key, part):
    return cluster_ids(key)[1]


def draw_scores(key, part):
    worker, firm_id, ordinal = cluster_ids(key)
    key = jax.random.fold_in(key, 7)
    subkeys = jax.random.split(key, 5)
    pair_id = 2 * worker + ordinal

    def effects(worker_one, pair_one, firm_one):
        worker_part = jax.random.normal(jax.random.fold_in(subkeys[0], worker_one), (K,))
        pair_part = jax.random.normal(jax.random.fold_in(subkeys[1], pair_one), (K,))
        firm_part = jax.random.normal(jax.random.fold_in(subkeys[2], firm_one), (K,))
        return 0.6 * worker_part + 0.5 * pair_part + 0.3 * firm_part
    shared = jax.vmap(effects)(worker, pair_id, firm_id)
    columns = jnp.exp(jax.random.uniform(subkeys[3], (K,), jnp.float32, -1.15, 1.15))
    noise = jax.random.normal(subkeys[4], (TOTAL, K))
    values = columns * (0.7 * noise + shared)
    return values.astype(jnp.float32).astype(jnp.bfloat16)


def setup_inputs(seed: int = 0) -> dict:
    seeds = jax.random.split(jax.random.key(seed), 4)
    scores = draw_scores(jax.random.fold_in(seeds[3], 71), 0)
    worker_ids = draw_worker_ids(jax.random.fold_in(seeds[3], 71), 0)
    firm_ids = draw_firm_ids(jax.random.fold_in(seeds[3], 71), 0)
    return {"scores": scores, "worker_ids": worker_ids, "firm_ids": firm_ids}


def gram(sums):
    return lax.dot_general(sums, sums, (((0,), (0,)), ((), ())), precision=lax.Precision.HIGHEST, preferred_element_type=jnp.float32)


def reference(scores, worker_ids, firm_ids):
    vectors = scores.astype(jnp.float32)
    first_table = jnp.full((WORKERS,), 2 ** 30, jnp.int32).at[worker_ids].min(firm_ids)
    first_firm = first_table[worker_ids].astype(jnp.int32)
    ordinal = (firm_ids != first_firm).astype(jnp.int32)
    pair_ids = (2 * worker_ids + ordinal).astype(jnp.int32)
    pair_sums = jax.ops.segment_sum(vectors, pair_ids, num_segments=2 * WORKERS)
    worker_sums = pair_sums[0::2] + pair_sums[1::2]
    firm_sums = jax.ops.segment_sum(vectors, firm_ids, num_segments=FIRMS)
    meat = gram(worker_sums) + gram(firm_sums) - gram(pair_sums)
    return meat * (1.0 / TOTAL)
```

```python
import jax
import jax.numpy as jnp
from jax import lax
from jax.sharding import PartitionSpec as P

LANES = 128


def equal_before(keys):
    index = jnp.arange(keys.shape[0], dtype=jnp.int32)
    same = (keys[:, None] == keys[None, :]) & (index[:, None] < index[None, :])
    return jnp.sum(same.astype(jnp.int32), axis=0)


def one_hot(targets, number):
    rows = lax.broadcasted_iota(jnp.int32, (number, targets.shape[0]), 0)
    return (rows == targets[None, :]).astype(jnp.bfloat16)


def placed_values(targets, values, number):
    rows = lax.broadcasted_iota(jnp.int32, (number, targets.shape[0]), 0)
    return jnp.max(jnp.where(rows == targets[None, :], values[None, :], -1), axis=1)


def dot(a, b):
    return jnp.dot(a, b, preferred_element_type=jnp.float32)


def solution(mesh):
    row_count, group_count = mesh.shape["rows"], mesh.shape["group"]
    classes = row_count * group_count
    everyone = ("rows", "group")
    workers_here = 65536 // classes
    firms_here = 32768 // classes
    firms = 32768

    def local(scores, worker_ids, firm_ids):
        local_rows, width = scores.shape
        capacity = 2 * local_rows // classes

        home = worker_ids % classes
        target = home * capacity + equal_before(home)
        code = (worker_ids // classes) * firms + firm_ids
        slot_codes = placed_values(target, code, classes * capacity)
        codes = lax.all_to_all(
            slot_codes.reshape(classes, capacity), everyone, 0, 0, tiled=True
        ).reshape(-1)
        packed = dot(one_hot(target, classes * capacity), scores).astype(jnp.bfloat16)
        got = lax.all_to_all(packed, everyone, 0, 0, tiled=True)

        used = codes >= 0
        worker = jnp.where(used, codes // firms, -1)
        firm = jnp.where(used, codes % firms, -1)
        table = lax.broadcasted_iota(jnp.int32, (workers_here, codes.shape[0]), 0) == worker[None, :]
        first = jnp.min(jnp.where(table, firm[None, :], 2**30), axis=1)
        row_first = jnp.max(jnp.where(table, first[:, None], -1), axis=0)
        pair = jnp.where(used, worker + workers_here * (firm != row_first).astype(jnp.int32), -1)
        pair_firm = placed_values(pair, firm, 2 * workers_here)
        firm_home = jnp.where(pair_firm >= 0, pair_firm % classes, -1)
        pair_slot = jnp.where(pair_firm >= 0, 2 * firm_home + equal_before(firm_home), -1)
        pair_rows = lax.broadcasted_iota(jnp.int32, (2 * workers_here, codes.shape[0]), 0)
        row_slot = jnp.max(jnp.where(pair_rows == pair[None, :], pair_slot[:, None], -1), axis=0)

        sent = dot(one_hot(row_slot, 2 * classes), got).astype(jnp.bfloat16)
        sent_firm = placed_values(pair_slot, pair_firm // classes, 2 * classes)
        tail = jnp.broadcast_to(sent_firm.astype(jnp.bfloat16)[:, None], (2 * classes, LANES))
        came = lax.all_to_all(
            jnp.concatenate([sent, tail], axis=1), everyone, 0, 0, tiled=True
        )
        pairs = dot(one_hot(pair, 2 * workers_here), got).astype(jnp.bfloat16)
        firm_local = came[:, width].astype(jnp.int32)
        firm_sums = dot(one_hot(firm_local, firms_here), came[:, :width]).astype(jnp.bfloat16)

        left = jnp.concatenate([pairs, firm_sums], axis=0)
        right = jnp.concatenate([pairs[workers_here:], pairs[:workers_here], firm_sums], axis=0)
        term = lax.dot_general(
            left, right, (((0,), (0,)), ((), ())), preferred_element_type=jnp.float32
        ).astype(jnp.bfloat16)
        block_rows, block_cols = width // row_count, width // group_count
        blocks = term.reshape(row_count, block_rows, group_count, block_cols)
        blocks = blocks.transpose(0, 2, 1, 3).reshape(classes, block_rows, block_cols)
        terms = lax.all_to_all(blocks, everyone, 0, 0, tiled=True)
        total = jnp.sum(terms.astype(jnp.float32), axis=0)
        return total * (1.0 / (classes * local_rows))

    placed = (P(everyone, None), P(everyone), P(everyone))
    return jax.shard_map(
        local, mesh=mesh, in_specs=placed, out_specs=P("rows", "group"), check_vma=False
    )
```

```python
import jax
import jax.numpy as jnp
from jax import lax
from jax.sharding import Mesh, PartitionSpec as P

AXES = ("x", "z", "core", "group")
EVERYONE = AXES
LANES = 128
FIRMS = 32768
WORKERS = 65536


def equal_before(keys):
    index = jnp.arange(keys.shape[0], dtype=jnp.int32)
    same = (keys[:, None] == keys[None, :]) & (index[:, None] < index[None, :])
    return jnp.sum(same.astype(jnp.int32), axis=0)


def one_hot(targets, number):
    rows = lax.broadcasted_iota(jnp.int32, (number, targets.shape[0]), 0)
    return (rows == targets[None, :]).astype(jnp.bfloat16)


def placed_values(targets, values, number):
    rows = lax.broadcasted_iota(jnp.int32, (number, targets.shape[0]), 0)
    return jnp.max(jnp.where(rows == targets[None, :], values[None, :], -1), axis=1)


def dot(a, b):
    return jnp.dot(a, b, preferred_element_type=jnp.float32)


def gram(a, b):
    return lax.dot_general(a, b, (((0,), (0,)), ((), ())), preferred_element_type=jnp.float32)


def swapped(value, axis, bit):
    size = lax.axis_size(axis)
    return lax.ppermute(value, axis, [(i, i ^ bit) for i in range(size)])


def exchange(blocks):
    classes, k = blocks.shape
    held = blocks.reshape(-1)
    before = 1
    for axis in AXES:
        bit = lax.axis_size(axis) // 2
        while bit:
            view = held.reshape(before, 2, -1)
            high = (lax.axis_index(axis) & bit) > 0
            keep = jnp.where(high, view[:, 1], view[:, 0])
            send = jnp.where(high, view[:, 0], view[:, 1])
            came = swapped(send, axis, bit)
            low_part = jnp.where(high, came, keep)
            high_part = jnp.where(high, keep, came)
            held = jnp.stack([low_part, high_part], axis=1).reshape(-1)
            before *= 2
            bit //= 2
    return held.reshape(classes, k)


def solution(mesh):
    row_count, group_count = mesh.shape["rows"], mesh.shape["group"]
    classes = row_count * group_count
    planes = row_count // 2
    fine = Mesh(mesh.devices.reshape(4, row_count // 8, 2, group_count), AXES)
    workers_here = WORKERS // classes
    firms_here = FIRMS // classes

    def local(scores, worker_ids, firm_ids):
        local_rows, width = scores.shape
        capacity = 2 * local_rows // classes
        core = lax.axis_index("core")

        home = worker_ids % classes
        target = home * capacity + equal_before(home)
        packed = dot(one_hot(target, classes * capacity), scores).astype(jnp.bfloat16)
        got = lax.all_to_all(packed, EVERYONE, 0, 0, tiled=True)
        code = (worker_ids // classes) * FIRMS + firm_ids
        slot_codes = placed_values(target, code, classes * capacity)
        codes = exchange(slot_codes.reshape(classes, capacity)).reshape(-1)

        used = codes >= 0
        worker = jnp.where(used, codes // FIRMS, -1)
        firm = jnp.where(used, codes % FIRMS, -1)
        table = lax.broadcasted_iota(jnp.int32, (workers_here, codes.shape[0]), 0) == worker[None, :]
        first = jnp.min(jnp.where(table, firm[None, :], 2**30), axis=1)
        row_first = jnp.max(jnp.where(table, first[:, None], -1), axis=0)
        pair = jnp.where(used, worker + workers_here * (firm != row_first).astype(jnp.int32), -1)
        pair_firm = placed_values(pair, firm, 2 * workers_here)
        firm_home = jnp.where(pair_firm >= 0, pair_firm % classes, -1)
        pair_slot = jnp.where(pair_firm >= 0, 2 * firm_home + equal_before(firm_home), -1)
        pair_rows = lax.broadcasted_iota(jnp.int32, (2 * workers_here, codes.shape[0]), 0)
        row_slot = jnp.max(jnp.where(pair_rows == pair[None, :], pair_slot[:, None], -1), axis=0)
        sent_firm = placed_values(pair_slot, pair_firm // classes, 2 * classes)

        sent = dot(one_hot(row_slot, 2 * classes), got).astype(jnp.bfloat16)
        tail = jnp.broadcast_to(sent_firm.astype(jnp.bfloat16)[:, None], (2 * classes, LANES))
        came = lax.all_to_all(
            jnp.concatenate([sent, tail], axis=1), EVERYONE, 0, 0, tiled=True
        )

        pairs = dot(one_hot(pair, 2 * workers_here), got).astype(jnp.bfloat16)
        more = swapped(pairs, "core", 1)
        half = workers_here
        left = jnp.concatenate([pairs, more], axis=0)
        right = jnp.concatenate([pairs[half:], pairs[:half], more[half:], more[:half]], axis=0)
        block_rows, block_cols = width // row_count, width // group_count
        picked = jnp.arange(width // 2, dtype=jnp.int32)
        picked = (picked // block_rows * 2 + core) * block_rows + picked % block_rows
        pick = one_hot(picked, width)
        left = dot(left, pick).astype(jnp.bfloat16)
        worker_terms = [
            gram(left, right[:, g * block_cols : (g + 1) * block_cols]) for g in range(group_count)
        ]

        came, worker_terms = lax.optimization_barrier((came, worker_terms))
        firm_local = came[:, width].astype(jnp.int32)
        firm_sums = dot(one_hot(firm_local, firms_here), came[:, :width])
        high = lax.optimization_barrier(firm_sums.astype(jnp.bfloat16))
        low = (firm_sums - high.astype(jnp.float32)).astype(jnp.bfloat16)
        firm_pair = jnp.concatenate([high, low], axis=0)
        firm_pair = jnp.concatenate([firm_pair, swapped(firm_pair, "core", 1)], axis=0)
        firm_left = dot(firm_pair, pick).astype(jnp.bfloat16)
        n = firms_here
        firm_left = jnp.concatenate([firm_left, firm_left[:n], firm_left[2 * n : 3 * n]], axis=0)
        firm_right = jnp.concatenate(
            [firm_pair[:n], firm_pair[:n], firm_pair[2 * n : 3 * n], firm_pair[2 * n : 3 * n],
             firm_pair[n : 2 * n], firm_pair[3 * n :]],
            axis=0,
        )
        terms = jnp.stack(
            [
                (worker_terms[g] + gram(firm_left, firm_right[:, g * block_cols : (g + 1) * block_cols])).astype(
                    jnp.bfloat16
                )
                for g in range(group_count)
            ]
        )
        terms = lax.all_to_all(terms, "group", 0, 0, tiled=True)
        wide = [terms[g].astype(jnp.float32) for g in range(group_count)]
        terms = sum(wide[1:], wide[0])
        terms = lax.all_to_all(
            terms.reshape(planes, block_rows, block_cols), ("x", "z"), 0, 0, tiled=True
        )
        total = jnp.sum(terms, axis=0)
        return total * (1.0 / (classes * local_rows))

    placed = (P(EVERYONE, None), P(EVERYONE), P(EVERYONE))
    return jax.shard_map(
        local, mesh=fine, in_specs=placed, out_specs=P(("x", "z", "core"), "group"), check_vma=False
    )
```

```python
import jax
import jax.numpy as jnp
from jax import lax
from jax.sharding import Mesh, PartitionSpec as P

AXES = ("x", "z", "core", "group")
EVERYONE = AXES
LANES = 128
FIRMS = 32768
WORKERS = 65536


def equal_before(keys):
    index = jnp.arange(keys.shape[0], dtype=jnp.int32)
    same = (keys[:, None] == keys[None, :]) & (index[:, None] < index[None, :])
    return jnp.sum(same.astype(jnp.int32), axis=0)


def one_hot(targets, number):
    rows = lax.broadcasted_iota(jnp.int32, (number, targets.shape[0]), 0)
    return (rows == targets[None, :]).astype(jnp.bfloat16)


def placed_values(targets, values, number):
    rows = lax.broadcasted_iota(jnp.int32, (number, targets.shape[0]), 0)
    return jnp.max(jnp.where(rows == targets[None, :], values[None, :], -1), axis=1)


def dot(a, b):
    return jnp.dot(a, b, preferred_element_type=jnp.float32)


def gram(a, b):
    return lax.dot_general(a, b, (((0,), (0,)), ((), ())), preferred_element_type=jnp.float32)


def swapped(value, axis, bit):
    size = lax.axis_size(axis)
    return lax.ppermute(value, axis, [(i, i ^ bit) for i in range(size)])


def exchange(blocks):
    k = blocks.shape[1]
    sizes = [lax.axis_size(axis) for axis in AXES]
    held = blocks.reshape(*sizes, k).transpose(1, 0, 2, 3, 4).reshape(sizes[1], -1)
    held = lax.all_to_all(held, "z", 0, 0, tiled=True).reshape(-1)
    before = sizes[1]
    for axis in ("x", "core", "group"):
        bit = lax.axis_size(axis) // 2
        while bit:
            view = held.reshape(before, 2, -1)
            high = (lax.axis_index(axis) & bit) > 0
            keep = jnp.where(high, view[:, 1], view[:, 0])
            send = jnp.where(high, view[:, 0], view[:, 1])
            came = swapped(send, axis, bit)
            low_part = jnp.where(high, came, keep)
            high_part = jnp.where(high, keep, came)
            held = jnp.stack([low_part, high_part], axis=1).reshape(-1)
            before *= 2
            bit //= 2
    held = held.reshape(sizes[1], sizes[0], -1).transpose(1, 0, 2)
    return held.reshape(-1)


def solution(mesh):
    row_count, group_count = mesh.shape["rows"], mesh.shape["group"]
    classes = row_count * group_count
    x_count, z_count = 4, row_count // 8
    fine = Mesh(mesh.devices.reshape(x_count, z_count, 2, group_count), AXES)
    workers_here = WORKERS // classes
    firms_here = FIRMS // classes

    def local(scores, worker_ids, firm_ids):
        local_rows, width = scores.shape
        capacity = 2 * local_rows // classes
        core = lax.axis_index("core")

        home = worker_ids % classes
        target = home * capacity + equal_before(home)
        packed = dot(one_hot(target, classes * capacity), scores).astype(jnp.bfloat16)
        got = lax.all_to_all(packed, EVERYONE, 0, 0, tiled=True)
        code = (worker_ids // classes) * FIRMS + firm_ids
        slot_codes = placed_values(target, code, classes * capacity)
        codes = exchange(slot_codes.reshape(classes, capacity))

        used = codes >= 0
        worker = jnp.where(used, codes // FIRMS, -1)
        firm = jnp.where(used, codes % FIRMS, -1)
        table = lax.broadcasted_iota(jnp.int32, (workers_here, codes.shape[0]), 0) == worker[None, :]
        first = jnp.min(jnp.where(table, firm[None, :], 2**30), axis=1)
        row_first = jnp.max(jnp.where(table, first[:, None], -1), axis=0)
        pair = jnp.where(used, worker + workers_here * (firm != row_first).astype(jnp.int32), -1)
        pair_firm = placed_values(pair, firm, 2 * workers_here)
        firm_home = jnp.where(pair_firm >= 0, pair_firm % classes, -1)
        pair_slot = jnp.where(pair_firm >= 0, 2 * firm_home + equal_before(firm_home), -1)
        pair_rows = lax.broadcasted_iota(jnp.int32, (2 * workers_here, codes.shape[0]), 0)
        row_slot = jnp.max(jnp.where(pair_rows == pair[None, :], pair_slot[:, None], -1), axis=0)
        sent_firm = placed_values(pair_slot, pair_firm // classes, 2 * classes)

        sent = dot(one_hot(row_slot, 2 * classes), got).astype(jnp.bfloat16)
        tail = jnp.broadcast_to(sent_firm.astype(jnp.bfloat16)[:, None], (2 * classes, LANES))
        came = lax.all_to_all(
            jnp.concatenate([sent, tail], axis=1), EVERYONE, 0, 0, tiled=True
        )

        half = workers_here
        other_slot = jnp.concatenate([pair_slot[half:], pair_slot[:half]])
        slots = jnp.arange(2 * classes, dtype=jnp.int32)
        has_pair = slots[:, None] == jnp.where(pair_slot >= 0, pair_slot, -1)[None, :]
        partner = jnp.max(jnp.where(has_pair, other_slot[None, :], -1), axis=1)
        mates = dot((partner[:, None] == slots[None, :]).astype(jnp.bfloat16), sent).astype(jnp.bfloat16)
        left = jnp.concatenate([sent, swapped(sent, "core", 1)], axis=0)
        right = jnp.concatenate([mates, swapped(mates, "core", 1)], axis=0)
        block_rows, block_cols = width // row_count, width // group_count
        picked = jnp.arange(width // 2, dtype=jnp.int32)
        picked = (picked // block_rows * 2 + core) * block_rows + picked % block_rows
        pick = one_hot(picked, width)
        left = dot(left, pick).astype(jnp.bfloat16)
        worker_terms = [
            gram(left, right[:, g * block_cols : (g + 1) * block_cols]) for g in range(group_count)
        ]

        came, worker_terms = lax.optimization_barrier((came, worker_terms))
        firm_local = came[:, width].astype(jnp.int32)
        firm_sums = dot(one_hot(firm_local, firms_here), came[:, :width])
        high = lax.optimization_barrier(firm_sums.astype(jnp.bfloat16))
        low = (firm_sums - high.astype(jnp.float32)).astype(jnp.bfloat16)
        firm_pair = jnp.concatenate([high, low], axis=0)
        firm_pair = jnp.concatenate([firm_pair, swapped(firm_pair, "core", 1)], axis=0)
        firm_left = dot(firm_pair, pick).astype(jnp.bfloat16)
        n = firms_here
        firm_left = jnp.concatenate([firm_left, firm_left[:n], firm_left[2 * n : 3 * n]], axis=0)
        firm_right = jnp.concatenate(
            [firm_pair[:n], firm_pair[:n], firm_pair[2 * n : 3 * n], firm_pair[2 * n : 3 * n],
             firm_pair[n : 2 * n], firm_pair[3 * n :]],
            axis=0,
        )
        terms = [
            (worker_terms[g] + gram(firm_left, firm_right[:, g * block_cols : (g + 1) * block_cols]))
            .astype(jnp.bfloat16)
            .reshape(x_count, -1, block_cols)
            for g in range(group_count)
        ]
        terms = jnp.stack(terms, axis=1).reshape(x_count * group_count, -1, block_cols)
        terms = lax.all_to_all(terms, ("x", "group"), 0, 0, tiled=True)
        wide = [terms[i].astype(jnp.float32) for i in range(x_count * group_count)]
        terms = sum(wide[1:], wide[0])
        terms = lax.all_to_all(
            terms.reshape(z_count, block_rows, block_cols), "z", 0, 0, tiled=True
        )
        total = sum([terms[i] for i in range(1, z_count)], terms[0])
        return total * (1.0 / (classes * local_rows))

    placed = (P(EVERYONE, None), P(EVERYONE), P(EVERYONE))
    return jax.shard_map(
        local, mesh=fine, in_specs=placed, out_specs=P(("x", "z", "core"), "group"), check_vma=False
    )
```

```python
import jax
import jax.numpy as jnp
from jax import lax
from jax.experimental import pallas as pl
from jax.experimental.pallas import tpu as pltpu
from jax.sharding import Mesh, PartitionSpec as P

LANES = 128
AXES = ("x", "z", "core", "group")
EVERYONE = AXES
FIRMS = 32768
WORKERS = 65536


def equal_before(keys):
    index = jnp.arange(keys.shape[0], dtype=jnp.int32)
    same = (keys[:, None] == keys[None, :]) & (index[:, None] < index[None, :])
    return jnp.sum(same.astype(jnp.int32), axis=0)


def one_hot(targets, number):
    rows = lax.broadcasted_iota(jnp.int32, (number, targets.shape[0]), 0)
    return (rows == targets[None, :]).astype(jnp.bfloat16)


def placed_values(targets, values, number):
    rows = lax.broadcasted_iota(jnp.int32, (number, targets.shape[0]), 0)
    return jnp.max(jnp.where(rows == targets[None, :], values[None, :], -1), axis=1)


def dot(a, b):
    return jnp.dot(a, b, preferred_element_type=jnp.float32)


def gram(a, b):
    return lax.dot_general(a, b, (((0,), (0,)), ((), ())), preferred_element_type=jnp.float32)


def swapped(value, axis, bit):
    size = lax.axis_size(axis)
    return lax.ppermute(value, axis, [(i, i ^ bit) for i in range(size)])


def swap_bits(held, before):
    shape = held.shape
    for axis in ("x", "core", "group"):
        bit = lax.axis_size(axis) // 2
        while bit:
            view = held.reshape(before, 2, -1)
            high = (lax.axis_index(axis) & bit) > 0
            keep = jnp.where(high, view[:, 1], view[:, 0])
            send = jnp.where(high, view[:, 0], view[:, 1])
            came = swapped(send, axis, bit)
            low_part = jnp.where(high, came, keep)
            high_part = jnp.where(high, keep, came)
            held = jnp.stack([low_part, high_part], axis=1)
            before *= 2
            bit //= 2
    return held.reshape(shape)


def all_terms(own, other, pick, worker_terms, row_parts, col_parts):
    firms, width = own.shape[0] // 2, own.shape[1]
    picked = pick.shape[0]
    cols = width // col_parts

    def kernel(own_ref, other_ref, pick_ref, terms_ref, out_ref, high_ref, low_ref, left_ref):
        g = pl.program_id(0)

        @pl.when(g == 0)
        def _():
            high_ref[:firms] = own_ref[:firms]
            high_ref[firms:] = other_ref[:firms]
            low_ref[:firms] = own_ref[firms:]
            low_ref[firms:] = other_ref[firms:]
            across = (((1,), (1,)), ((), ()))
            for at, ref in ((0, high_ref), (2 * firms, low_ref)):
                left_ref[:, at : at + 2 * firms] = lax.dot_general(
                    pick_ref[...], ref[...], across, preferred_element_type=jnp.float32
                ).astype(jnp.bfloat16)

        here = pl.ds(pl.multiple_of(g * cols, cols), cols)
        high, low = high_ref[:, here], low_ref[:, here]
        left_high, left_low = left_ref[:, : 2 * firms], left_ref[:, 2 * firms :]
        sums = terms_ref[...] + (dot(left_high, low) + dot(left_low, high)) + dot(left_high, high)
        out_ref[...] = sums.astype(jnp.bfloat16).reshape(out_ref.shape)

    return pl.pallas_call(
        kernel,
        grid=(col_parts,),
        in_specs=[
            pl.BlockSpec((2 * firms, width), lambda g: (0, 0)),
            pl.BlockSpec((2 * firms, width), lambda g: (0, 0)),
            pl.BlockSpec((picked, width), lambda g: (0, 0)),
            pl.BlockSpec((picked, cols), lambda g: (0, g)),
        ],
        out_specs=pl.BlockSpec((row_parts, 1, picked // row_parts, cols), lambda g: (0, g, 0, 0)),
        out_shape=jax.ShapeDtypeStruct((row_parts, col_parts, picked // row_parts, cols), jnp.bfloat16),
        scratch_shapes=[
            pltpu.VMEM((2 * firms, width), jnp.bfloat16),
            pltpu.VMEM((2 * firms, width), jnp.bfloat16),
            pltpu.VMEM((picked, 4 * firms), jnp.bfloat16),
        ],
        compiler_params=pltpu.CompilerParams(vmem_limit_bytes=24 * 1024 * 1024),
        cost_estimate=pl.CostEstimate(
            flops=2 * picked * width * 10 * firms, bytes_accessed=6 * 1024 * 1024, transcendentals=0
        ),
    )(own, other, pick, worker_terms)


def solution(mesh):
    row_count, group_count = mesh.shape["rows"], mesh.shape["group"]
    classes = row_count * group_count
    x_count, z_count = 4, row_count // 8
    fine = Mesh(mesh.devices.reshape(x_count, z_count, 2, group_count), AXES)
    workers_here = WORKERS // classes
    firms_here = FIRMS // classes

    def local(scores, worker_ids, firm_ids):
        local_rows, width = scores.shape
        capacity = 2 * local_rows // classes
        core = lax.axis_index("core")

        raw = worker_ids * FIRMS + firm_ids
        raw = lax.all_to_all(
            jnp.broadcast_to(raw[None, :], (z_count, local_rows)), "z", 0, 0, tiled=True
        )

        home = worker_ids % classes
        target = home * capacity + equal_before(home)
        packed = dot(one_hot(target, classes * capacity), scores).astype(jnp.bfloat16)
        packed, raw = lax.optimization_barrier((packed, raw))
        got = lax.all_to_all(packed, EVERYONE, 0, 0, tiled=True)

        inner = 2 * group_count
        raw_worker = raw // FIRMS
        raw_home = raw_worker % classes
        mine = (raw_home // inner) % z_count == lax.axis_index("z")
        across = (raw_home // (inner * z_count)) * inner + raw_home % inner
        across = jnp.where(mine, across, -1)
        slot = jnp.where(mine, across * capacity + jax.vmap(equal_before)(across), -1)
        raw_code = (raw_worker // classes) * FIRMS + raw % FIRMS
        slot_codes = jax.vmap(lambda t, v: placed_values(t, v, x_count * inner * capacity))(slot, raw_code)
        codes = swap_bits(slot_codes, z_count)
        codes = codes.reshape(z_count, x_count, -1).transpose(1, 0, 2).reshape(-1)

        used = codes >= 0
        worker = jnp.where(used, codes // FIRMS, -1)
        firm = jnp.where(used, codes % FIRMS, -1)
        table = lax.broadcasted_iota(jnp.int32, (workers_here, codes.shape[0]), 0) == worker[None, :]
        first = jnp.min(jnp.where(table, firm[None, :], 2**30), axis=1)
        row_first = jnp.max(jnp.where(table, first[:, None], -1), axis=0)
        pair = jnp.where(used, worker + workers_here * (firm != row_first).astype(jnp.int32), -1)
        pair_firm = placed_values(pair, firm, 2 * workers_here)
        firm_home = jnp.where(pair_firm >= 0, pair_firm % classes, -1)
        pair_slot = jnp.where(pair_firm >= 0, 2 * firm_home + equal_before(firm_home), -1)
        pair_rows = lax.broadcasted_iota(jnp.int32, (2 * workers_here, codes.shape[0]), 0)
        row_slot = jnp.max(jnp.where(pair_rows == pair[None, :], pair_slot[:, None], -1), axis=0)
        sent_firm = placed_values(pair_slot, pair_firm // classes, 2 * classes)

        to_slots, got = lax.optimization_barrier((one_hot(row_slot, 2 * classes), got))
        sent = dot(to_slots, got).astype(jnp.bfloat16)
        tail = jnp.broadcast_to(sent_firm.astype(jnp.bfloat16)[:, None], (2 * classes, LANES))
        came = lax.all_to_all(
            jnp.concatenate([sent, tail], axis=1), EVERYONE, 0, 0, tiled=True
        )

        half = workers_here
        other_slot = jnp.concatenate([pair_slot[half:], pair_slot[:half]])
        slots = jnp.arange(2 * classes, dtype=jnp.int32)
        has_pair = slots[:, None] == jnp.where(pair_slot >= 0, pair_slot, -1)[None, :]
        partner = jnp.max(jnp.where(has_pair, other_slot[None, :], -1), axis=1)
        mates = dot((partner[:, None] == slots[None, :]).astype(jnp.bfloat16), sent).astype(jnp.bfloat16)
        left = jnp.concatenate([sent, swapped(sent, "core", 1)], axis=0)
        right = jnp.concatenate([mates, swapped(mates, "core", 1)], axis=0)
        block_rows, block_cols = width // row_count, width // group_count
        picked = jnp.arange(width // 2, dtype=jnp.int32)
        picked = (picked // block_rows * 2 + core) * block_rows + picked % block_rows
        columns = jnp.arange(width, dtype=jnp.int32)
        pick = (picked[:, None] == columns[None, :]).astype(jnp.bfloat16)
        left = lax.dot_general(
            left, pick, (((1,), (1,)), ((), ())), preferred_element_type=jnp.float32
        ).astype(jnp.bfloat16)
        worker_terms = gram(left, right)

        came, worker_terms, pick = lax.optimization_barrier((came, worker_terms, pick))
        firm_names = jnp.arange(firms_here, dtype=jnp.float32).astype(jnp.bfloat16)
        firm_hits = (came[:, width:] == firm_names[None, :]).astype(jnp.bfloat16)
        firm_sums = gram(firm_hits, came[:, :width])
        high = lax.optimization_barrier(firm_sums.astype(jnp.bfloat16))
        low = (firm_sums - high.astype(jnp.float32)).astype(jnp.bfloat16)
        firm_pair = jnp.concatenate([high, low], axis=0)
        terms = all_terms(
            firm_pair, swapped(firm_pair, "core", 1), pick, worker_terms, x_count, group_count
        )
        terms = terms.reshape(x_count * group_count, -1, block_cols)
        terms = lax.all_to_all(terms, ("x", "group"), 0, 0, tiled=True)
        wide = [terms[i].astype(jnp.float32) for i in range(x_count * group_count)]
        terms = sum(wide[1:], wide[0])
        terms = lax.all_to_all(
            terms.reshape(z_count, block_rows, block_cols), "z", 0, 0, tiled=True
        )
        total = sum([terms[i] for i in range(1, z_count)], terms[0])
        return total * (1.0 / (classes * local_rows))

    placed = (P(EVERYONE, None), P(EVERYONE), P(EVERYONE))
    return jax.shard_map(
        local, mesh=fine, in_specs=placed, out_specs=P(("x", "z", "core"), "group"), check_vma=False
    )
```

```python
import jax
import jax.numpy as jnp
from jax import lax
from jax.experimental import pallas as pl
from jax.experimental.pallas import tpu as pltpu
from jax.sharding import Mesh, PartitionSpec as P

LANES = 128
AXES = ("x", "z", "core", "group")
EVERYONE = AXES
FIRMS = 32768
WORKERS = 65536


def equal_before(keys):
    index = jnp.arange(keys.shape[0], dtype=jnp.int32)
    same = (keys[:, None] == keys[None, :]) & (index[:, None] < index[None, :])
    return jnp.sum(same.astype(jnp.int32), axis=0)


def one_hot(targets, number):
    rows = lax.broadcasted_iota(jnp.int32, (number, targets.shape[0]), 0)
    return (rows == targets[None, :]).astype(jnp.bfloat16)


def placed_values(targets, values, number):
    rows = lax.broadcasted_iota(jnp.int32, (number, targets.shape[0]), 0)
    return jnp.max(jnp.where(rows == targets[None, :], values[None, :], -1), axis=1)


def dot(a, b):
    return jnp.dot(a, b, preferred_element_type=jnp.float32)


def gram(a, b):
    return lax.dot_general(a, b, (((0,), (0,)), ((), ())), preferred_element_type=jnp.float32)


def swapped(value, axis, bit):
    size = lax.axis_size(axis)
    return lax.ppermute(value, axis, [(i, i ^ bit) for i in range(size)])


def swap_bits(held, before):
    shape = held.shape
    for axis in ("x", "core", "group"):
        bit = lax.axis_size(axis) // 2
        while bit:
            view = held.reshape(before, 2, -1)
            high = (lax.axis_index(axis) & bit) > 0
            keep = jnp.where(high, view[:, 1], view[:, 0])
            send = jnp.where(high, view[:, 0], view[:, 1])
            came = swapped(send, axis, bit)
            low_part = jnp.where(high, came, keep)
            high_part = jnp.where(high, keep, came)
            held = jnp.stack([low_part, high_part], axis=1)
            before *= 2
            bit //= 2
    return held.reshape(shape)


def pack_rows(targets, rows, slots):
    count, width = rows.shape
    step = 256

    def kernel(targets_ref, rows_ref, out_ref):
        first = pl.program_id(0) * step
        names = lax.broadcasted_iota(jnp.int32, (step, count), 0) + first
        hits = (names == targets_ref[...]).astype(jnp.float32).astype(jnp.bfloat16)
        out_ref[...] = dot(hits, rows_ref[...]).astype(jnp.bfloat16)

    return pl.pallas_call(
        kernel,
        grid=(slots // step,),
        in_specs=[
            pl.BlockSpec((1, count), lambda i: (0, 0)),
            pl.BlockSpec((count, width), lambda i: (0, 0)),
        ],
        out_specs=pl.BlockSpec((step, width), lambda i: (i, 0)),
        out_shape=jax.ShapeDtypeStruct((slots, width), jnp.bfloat16),
        compiler_params=pltpu.CompilerParams(vmem_limit_bytes=60 * 1024 * 1024),
        cost_estimate=pl.CostEstimate(
            flops=2 * slots * count * width, bytes_accessed=6 * 1024 * 1024, transcendentals=0
        ),
    )(targets[None, :], rows)


def slot_sums(slots_of, rows, tail):
    count, width = rows.shape
    slots, lanes = tail.shape
    step = 256

    def kernel(slots_ref, rows_ref, tail_ref, out_ref, hits_ref):
        j = pl.program_id(0)

        @pl.when(j == 0)
        def _():
            names = lax.broadcasted_iota(jnp.int32, (slots, step), 0)
            for at in range(0, count, step):
                hits = names == slots_ref[:, at : at + step]
                hits_ref[:, at : at + step] = hits.astype(jnp.float32).astype(jnp.bfloat16)
            out_ref[:, width:] = tail_ref[...]

        here = pl.ds(pl.multiple_of(j * step, step), step)
        out_ref[:, here] = dot(hits_ref[...], rows_ref[...]).astype(jnp.bfloat16)

    return pl.pallas_call(
        kernel,
        grid=(width // step,),
        in_specs=[
            pl.BlockSpec((1, count), lambda j: (0, 0)),
            pl.BlockSpec((count, step), lambda j: (0, j)),
            pl.BlockSpec((slots, lanes), lambda j: (0, 0)),
        ],
        out_specs=pl.BlockSpec((slots, width + lanes), lambda j: (0, 0)),
        out_shape=jax.ShapeDtypeStruct((slots, width + lanes), jnp.bfloat16),
        scratch_shapes=[pltpu.VMEM((slots, count), jnp.bfloat16)],
        compiler_params=pltpu.CompilerParams(vmem_limit_bytes=16 * 1024 * 1024),
        cost_estimate=pl.CostEstimate(
            flops=2 * slots * count * width, bytes_accessed=6 * 1024 * 1024, transcendentals=0
        ),
    )(slots_of[None, :], rows, tail)


def firm_halves(came, firms, width):
    count, lanes = came.shape[0], came.shape[1] - width

    def kernel(came_ref, out_ref):
        names = lax.broadcasted_iota(jnp.int32, (count, lanes), 1).astype(jnp.float32)
        hits = (came_ref[:, width:].astype(jnp.float32) == names).astype(jnp.float32).astype(jnp.bfloat16)
        sums = gram(hits, came_ref[:, :width])
        high = sums.astype(jnp.bfloat16)
        out_ref[:firms] = high
        out_ref[firms:] = (sums - high.astype(jnp.float32)).astype(jnp.bfloat16)

    return pl.pallas_call(
        kernel,
        out_shape=jax.ShapeDtypeStruct((2 * firms, width), jnp.bfloat16),
        compiler_params=pltpu.CompilerParams(vmem_limit_bytes=12 * 1024 * 1024),
        cost_estimate=pl.CostEstimate(
            flops=2 * count * firms * width, bytes_accessed=2 * 1024 * 1024, transcendentals=0
        ),
    )(came)


def all_terms(own, other, pick, worker_terms, row_parts, col_parts):
    firms, width = own.shape[0] // 2, own.shape[1]
    picked = pick.shape[0]
    cols = width // col_parts

    def kernel(own_ref, other_ref, pick_ref, terms_ref, out_ref, high_ref, low_ref, left_ref):
        g = pl.program_id(0)

        @pl.when(g == 0)
        def _():
            high_ref[:firms] = own_ref[:firms]
            high_ref[firms:] = other_ref[:firms]
            low_ref[:firms] = own_ref[firms:]
            low_ref[firms:] = other_ref[firms:]
            across = (((1,), (1,)), ((), ()))
            for at, ref in ((0, high_ref), (2 * firms, low_ref)):
                left_ref[:, at : at + 2 * firms] = lax.dot_general(
                    pick_ref[...], ref[...], across, preferred_element_type=jnp.float32
                ).astype(jnp.bfloat16)

        here = pl.ds(pl.multiple_of(g * cols, cols), cols)
        high, low = high_ref[:, here], low_ref[:, here]
        left_high, left_low = left_ref[:, : 2 * firms], left_ref[:, 2 * firms :]
        sums = terms_ref[...] + (dot(left_high, low) + dot(left_low, high)) + dot(left_high, high)
        out_ref[...] = sums.astype(jnp.bfloat16).reshape(out_ref.shape)

    return pl.pallas_call(
        kernel,
        grid=(col_parts,),
        in_specs=[
            pl.BlockSpec((2 * firms, width), lambda g: (0, 0)),
            pl.BlockSpec((2 * firms, width), lambda g: (0, 0)),
            pl.BlockSpec((picked, width), lambda g: (0, 0)),
            pl.BlockSpec((picked, cols), lambda g: (0, g)),
        ],
        out_specs=pl.BlockSpec((row_parts, 1, picked // row_parts, cols), lambda g: (0, g, 0, 0)),
        out_shape=jax.ShapeDtypeStruct((row_parts, col_parts, picked // row_parts, cols), jnp.bfloat16),
        scratch_shapes=[
            pltpu.VMEM((2 * firms, width), jnp.bfloat16),
            pltpu.VMEM((2 * firms, width), jnp.bfloat16),
            pltpu.VMEM((picked, 4 * firms), jnp.bfloat16),
        ],
        compiler_params=pltpu.CompilerParams(vmem_limit_bytes=12 * 1024 * 1024),
        cost_estimate=pl.CostEstimate(
            flops=2 * picked * width * 10 * firms, bytes_accessed=6 * 1024 * 1024, transcendentals=0
        ),
    )(own, other, pick, worker_terms)


def solution(mesh):
    row_count, group_count = mesh.shape["rows"], mesh.shape["group"]
    classes = row_count * group_count
    x_count, z_count = 4, row_count // 8
    fine = Mesh(mesh.devices.reshape(x_count, z_count, 2, group_count), AXES)
    workers_here = WORKERS // classes
    firms_here = FIRMS // classes

    def local(scores, worker_ids, firm_ids):
        local_rows, width = scores.shape
        capacity = 2 * local_rows // classes
        core = lax.axis_index("core")

        raw = worker_ids * FIRMS + firm_ids
        raw = lax.all_to_all(
            jnp.broadcast_to(raw[None, :], (z_count, local_rows)), "z", 0, 0, tiled=True
        )

        home = worker_ids % classes
        target = home * capacity + equal_before(home)
        packed = pack_rows(target, scores, classes * capacity)
        packed, raw = lax.optimization_barrier((packed, raw))
        got = lax.all_to_all(packed, EVERYONE, 0, 0, tiled=True)

        inner = 2 * group_count
        raw_worker = raw // FIRMS
        raw_home = raw_worker % classes
        mine = (raw_home // inner) % z_count == lax.axis_index("z")
        across = (raw_home // (inner * z_count)) * inner + raw_home % inner
        across = jnp.where(mine, across, -1)
        slot = jnp.where(mine, across * capacity + jax.vmap(equal_before)(across), -1)
        raw_code = (raw_worker // classes) * FIRMS + raw % FIRMS
        slot_codes = jax.vmap(lambda t, v: placed_values(t, v, x_count * inner * capacity))(slot, raw_code)
        codes = swap_bits(slot_codes, z_count)
        codes = codes.reshape(z_count, x_count, -1).transpose(1, 0, 2).reshape(-1)

        used = codes >= 0
        worker = jnp.where(used, codes // FIRMS, -1)
        firm = jnp.where(used, codes % FIRMS, -1)
        table = lax.broadcasted_iota(jnp.int32, (workers_here, codes.shape[0]), 0) == worker[None, :]
        first = jnp.min(jnp.where(table, firm[None, :], 2**30), axis=1)
        row_first = jnp.max(jnp.where(table, first[:, None], -1), axis=0)
        pair = jnp.where(used, worker + workers_here * (firm != row_first).astype(jnp.int32), -1)
        pair_firm = placed_values(pair, firm, 2 * workers_here)
        firm_home = jnp.where(pair_firm >= 0, pair_firm % classes, -1)
        pair_slot = jnp.where(pair_firm >= 0, 2 * firm_home + equal_before(firm_home), -1)
        pair_rows = lax.broadcasted_iota(jnp.int32, (2 * workers_here, codes.shape[0]), 0)
        row_slot = jnp.max(jnp.where(pair_rows == pair[None, :], pair_slot[:, None], -1), axis=0)
        sent_firm = placed_values(pair_slot, pair_firm // classes, 2 * classes)

        tail = jnp.broadcast_to(sent_firm.astype(jnp.bfloat16)[:, None], (2 * classes, LANES))
        tail, row_slot, got = lax.optimization_barrier((tail, row_slot, got))
        sent = slot_sums(row_slot, got, tail)
        came = lax.all_to_all(sent, EVERYONE, 0, 0, tiled=True)
        sent = sent[:, :width]

        half = workers_here
        other_slot = jnp.concatenate([pair_slot[half:], pair_slot[:half]])
        slots = jnp.arange(2 * classes, dtype=jnp.int32)
        has_pair = slots[:, None] == jnp.where(pair_slot >= 0, pair_slot, -1)[None, :]
        partner = jnp.max(jnp.where(has_pair, other_slot[None, :], -1), axis=1)
        mates = dot((partner[:, None] == slots[None, :]).astype(jnp.bfloat16), sent).astype(jnp.bfloat16)
        left = jnp.concatenate([sent, swapped(sent, "core", 1)], axis=0)
        right = jnp.concatenate([mates, swapped(mates, "core", 1)], axis=0)
        block_rows, block_cols = width // row_count, width // group_count
        picked = jnp.arange(width // 2, dtype=jnp.int32)
        picked = (picked // block_rows * 2 + core) * block_rows + picked % block_rows
        columns = jnp.arange(width, dtype=jnp.int32)
        pick = (picked[:, None] == columns[None, :]).astype(jnp.bfloat16)
        left = lax.dot_general(
            left, pick, (((1,), (1,)), ((), ())), preferred_element_type=jnp.float32
        ).astype(jnp.bfloat16)
        worker_terms = gram(left, right)

        came, worker_terms, pick = lax.optimization_barrier((came, worker_terms, pick))
        firm_pair = firm_halves(came, firms_here, width)
        terms = all_terms(
            firm_pair, swapped(firm_pair, "core", 1), pick, worker_terms, x_count, group_count
        )
        terms = terms.reshape(x_count * group_count, -1, block_cols)
        terms = lax.all_to_all(terms, ("x", "group"), 0, 0, tiled=True)
        wide = [terms[i].astype(jnp.float32) for i in range(x_count * group_count)]
        terms = sum(wide[1:], wide[0])
        terms = lax.all_to_all(
            terms.reshape(z_count, block_rows, block_cols), "z", 0, 0, tiled=True
        )
        total = sum([terms[i] for i in range(1, z_count)], terms[0])
        return total * (1.0 / (classes * local_rows))

    placed = (P(EVERYONE, None), P(EVERYONE), P(EVERYONE))
    return jax.shard_map(
        local, mesh=fine, in_specs=placed, out_specs=P(("x", "z", "core"), "group"), check_vma=False
    )
```

```python
import jax
import jax.numpy as jnp
from jax import lax
from jax.experimental import pallas as pl
from jax.experimental.pallas import tpu as pltpu
from jax.sharding import Mesh, PartitionSpec as P

LANES = 128
AXES = ("x", "z", "core", "group")
EVERYONE = AXES
FIRMS = 32768
WORKERS = 65536


def equal_before(keys):
    index = jnp.arange(keys.shape[0], dtype=jnp.int32)
    same = (keys[:, None] == keys[None, :]) & (index[:, None] < index[None, :])
    return jnp.sum(same.astype(jnp.int32), axis=0)


def one_hot(targets, number):
    rows = lax.broadcasted_iota(jnp.int32, (number, targets.shape[0]), 0)
    return (rows == targets[None, :]).astype(jnp.bfloat16)


def placed_values(targets, values, number):
    rows = lax.broadcasted_iota(jnp.int32, (number, targets.shape[0]), 0)
    return jnp.max(jnp.where(rows == targets[None, :], values[None, :], -1), axis=1)


def dot(a, b):
    return jnp.dot(a, b, preferred_element_type=jnp.float32)


def gram(a, b):
    return lax.dot_general(a, b, (((0,), (0,)), ((), ())), preferred_element_type=jnp.float32)


def swapped(value, axis, bit):
    size = lax.axis_size(axis)
    return lax.ppermute(value, axis, [(i, i ^ bit) for i in range(size)])


def swap_bits(held, before):
    shape = held.shape
    for axis in ("x", "core", "group"):
        bit = lax.axis_size(axis) // 2
        while bit:
            view = held.reshape(before, 2, -1)
            high = (lax.axis_index(axis) & bit) > 0
            keep = jnp.where(high, view[:, 1], view[:, 0])
            send = jnp.where(high, view[:, 0], view[:, 1])
            came = swapped(send, axis, bit)
            low_part = jnp.where(high, came, keep)
            high_part = jnp.where(high, keep, came)
            held = jnp.stack([low_part, high_part], axis=1)
            before *= 2
            bit //= 2
    return held.reshape(shape)


def pack_rows(targets, rows, slots):
    count, width = rows.shape
    step = 512

    def kernel(targets_ref, rows_ref, out_ref):
        first = pl.program_id(0) * step
        names = lax.broadcasted_iota(jnp.int32, (step, count), 0) + first
        hits = (names == targets_ref[...]).astype(jnp.float32).astype(jnp.bfloat16)
        out_ref[...] = dot(hits, rows_ref[...]).astype(jnp.bfloat16)

    return pl.pallas_call(
        kernel,
        grid=(slots // step,),
        in_specs=[
            pl.BlockSpec((1, count), lambda i: (0, 0)),
            pl.BlockSpec((count, width), lambda i: (0, 0)),
        ],
        out_specs=pl.BlockSpec((step, width), lambda i: (i, 0)),
        out_shape=jax.ShapeDtypeStruct((slots, width), jnp.bfloat16),
        compiler_params=pltpu.CompilerParams(vmem_limit_bytes=60 * 1024 * 1024),
        cost_estimate=pl.CostEstimate(
            flops=2 * slots * count * width, bytes_accessed=6 * 1024 * 1024, transcendentals=0
        ),
    )(targets[None, :], rows)


def slot_sums(slots_of, rows, tail):
    count, width = rows.shape
    slots, lanes = tail.shape
    step = 512

    def kernel(slots_ref, rows_ref, tail_ref, out_ref, hits_ref):
        j = pl.program_id(0)

        @pl.when(j == 0)
        def _():
            names = lax.broadcasted_iota(jnp.int32, (slots, step), 0)
            for at in range(0, count, step):
                hits = names == slots_ref[:, at : at + step]
                hits_ref[:, at : at + step] = hits.astype(jnp.float32).astype(jnp.bfloat16)
            out_ref[:, width:] = tail_ref[...]

        here = pl.ds(pl.multiple_of(j * step, step), step)
        out_ref[:, here] = dot(hits_ref[...], rows_ref[...]).astype(jnp.bfloat16)

    return pl.pallas_call(
        kernel,
        grid=(width // step,),
        in_specs=[
            pl.BlockSpec((1, count), lambda j: (0, 0)),
            pl.BlockSpec((count, step), lambda j: (0, j)),
            pl.BlockSpec((slots, lanes), lambda j: (0, 0)),
        ],
        out_specs=pl.BlockSpec((slots, width + lanes), lambda j: (0, 0)),
        out_shape=jax.ShapeDtypeStruct((slots, width + lanes), jnp.bfloat16),
        scratch_shapes=[pltpu.VMEM((slots, count), jnp.bfloat16)],
        compiler_params=pltpu.CompilerParams(vmem_limit_bytes=16 * 1024 * 1024),
        cost_estimate=pl.CostEstimate(
            flops=2 * slots * count * width, bytes_accessed=6 * 1024 * 1024, transcendentals=0
        ),
    )(slots_of[None, :], rows, tail)


def firm_halves(came, firms, width):
    count, lanes = came.shape[0], came.shape[1] - width

    def kernel(came_ref, out_ref):
        names = lax.broadcasted_iota(jnp.int32, (count, lanes), 1).astype(jnp.float32)
        hits = (came_ref[:, width:].astype(jnp.float32) == names).astype(jnp.float32).astype(jnp.bfloat16)
        sums = gram(hits, came_ref[:, :width])
        high = sums.astype(jnp.bfloat16)
        out_ref[:firms] = high
        out_ref[firms:] = (sums - high.astype(jnp.float32)).astype(jnp.bfloat16)

    return pl.pallas_call(
        kernel,
        out_shape=jax.ShapeDtypeStruct((2 * firms, width), jnp.bfloat16),
        compiler_params=pltpu.CompilerParams(vmem_limit_bytes=12 * 1024 * 1024),
        cost_estimate=pl.CostEstimate(
            flops=2 * count * firms * width, bytes_accessed=2 * 1024 * 1024, transcendentals=0
        ),
    )(came)


def all_terms(own, other, pick, worker_terms, row_parts, col_parts):
    firms, width = own.shape[0] // 2, own.shape[1]
    picked = pick.shape[0]
    cols = width // col_parts

    def kernel(own_ref, other_ref, pick_ref, terms_ref, out_ref, high_ref, low_ref, left_ref):
        g = pl.program_id(0)

        @pl.when(g == 0)
        def _():
            high_ref[:firms] = own_ref[:firms]
            high_ref[firms:] = other_ref[:firms]
            low_ref[:firms] = own_ref[firms:]
            low_ref[firms:] = other_ref[firms:]
            across = (((1,), (1,)), ((), ()))
            for at, ref in ((0, high_ref), (2 * firms, low_ref)):
                left_ref[:, at : at + 2 * firms] = lax.dot_general(
                    pick_ref[...], ref[...], across, preferred_element_type=jnp.float32
                ).astype(jnp.bfloat16)

        here = pl.ds(pl.multiple_of(g * cols, cols), cols)
        high, low = high_ref[:, here], low_ref[:, here]
        left_high, left_low = left_ref[:, : 2 * firms], left_ref[:, 2 * firms :]
        sums = terms_ref[...] + (dot(left_high, low) + dot(left_low, high)) + dot(left_high, high)
        out_ref[...] = sums.astype(jnp.bfloat16).reshape(out_ref.shape)

    return pl.pallas_call(
        kernel,
        grid=(col_parts,),
        in_specs=[
            pl.BlockSpec((2 * firms, width), lambda g: (0, 0)),
            pl.BlockSpec((2 * firms, width), lambda g: (0, 0)),
            pl.BlockSpec((picked, width), lambda g: (0, 0)),
            pl.BlockSpec((picked, cols), lambda g: (0, g)),
        ],
        out_specs=pl.BlockSpec((row_parts, 1, picked // row_parts, cols), lambda g: (0, g, 0, 0)),
        out_shape=jax.ShapeDtypeStruct((row_parts, col_parts, picked // row_parts, cols), jnp.bfloat16),
        scratch_shapes=[
            pltpu.VMEM((2 * firms, width), jnp.bfloat16),
            pltpu.VMEM((2 * firms, width), jnp.bfloat16),
            pltpu.VMEM((picked, 4 * firms), jnp.bfloat16),
        ],
        compiler_params=pltpu.CompilerParams(vmem_limit_bytes=12 * 1024 * 1024),
        cost_estimate=pl.CostEstimate(
            flops=2 * picked * width * 10 * firms, bytes_accessed=6 * 1024 * 1024, transcendentals=0
        ),
    )(own, other, pick, worker_terms)


def solution(mesh):
    row_count, group_count = mesh.shape["rows"], mesh.shape["group"]
    classes = row_count * group_count
    x_count, z_count = 4, row_count // 8
    fine = Mesh(mesh.devices.reshape(x_count, z_count, 2, group_count), AXES)
    workers_here = WORKERS // classes
    firms_here = FIRMS // classes

    def local(scores, worker_ids, firm_ids):
        local_rows, width = scores.shape
        capacity = 2 * local_rows // classes
        core = lax.axis_index("core")

        raw = jnp.broadcast_to((worker_ids * FIRMS + firm_ids)[None, :], (z_count, local_rows))
        raw, worker_ids = lax.optimization_barrier((raw, worker_ids))
        raw = lax.all_to_all(raw, "z", 0, 0, tiled=True)

        home = worker_ids % classes
        target = home * capacity + equal_before(home)
        packed = pack_rows(target, scores, classes * capacity)
        packed, raw = lax.optimization_barrier((packed, raw))
        got = lax.all_to_all(packed, EVERYONE, 0, 0, tiled=True)

        inner = 2 * group_count
        raw_worker = raw // FIRMS
        raw_home = raw_worker % classes
        mine = (raw_home // inner) % z_count == lax.axis_index("z")
        across = (raw_home // (inner * z_count)) * inner + raw_home % inner
        across = jnp.where(mine, across, -1)
        slot = jnp.where(mine, across * capacity + jax.vmap(equal_before)(across), -1)
        raw_code = (raw_worker // classes) * FIRMS + raw % FIRMS
        slot_codes = jax.vmap(lambda t, v: placed_values(t, v, x_count * inner * capacity))(slot, raw_code)
        codes = swap_bits(slot_codes, z_count)
        codes = codes.reshape(z_count, x_count, -1).transpose(1, 0, 2).reshape(-1)

        used = codes >= 0
        worker = jnp.where(used, codes // FIRMS, -1)
        firm = jnp.where(used, codes % FIRMS, -1)
        table = lax.broadcasted_iota(jnp.int32, (workers_here, codes.shape[0]), 0) == worker[None, :]
        first = jnp.min(jnp.where(table, firm[None, :], 2**30), axis=1)
        row_first = jnp.max(jnp.where(table, first[:, None], -1), axis=0)
        pair = jnp.where(used, worker + workers_here * (firm != row_first).astype(jnp.int32), -1)
        pair_firm = placed_values(pair, firm, 2 * workers_here)
        firm_home = jnp.where(pair_firm >= 0, pair_firm % classes, -1)
        pair_slot = jnp.where(pair_firm >= 0, 2 * firm_home + equal_before(firm_home), -1)
        pair_rows = lax.broadcasted_iota(jnp.int32, (2 * workers_here, codes.shape[0]), 0)
        row_slot = jnp.max(jnp.where(pair_rows == pair[None, :], pair_slot[:, None], -1), axis=0)
        sent_firm = placed_values(pair_slot, pair_firm // classes, 2 * classes)

        tail = jnp.broadcast_to(sent_firm.astype(jnp.bfloat16)[:, None], (2 * classes, LANES))
        tail, row_slot, got = lax.optimization_barrier((tail, row_slot, got))
        sent = slot_sums(row_slot, got, tail)
        came = lax.all_to_all(sent, EVERYONE, 0, 0, tiled=True)
        sent = sent[:, :width]

        half = workers_here
        other_slot = jnp.concatenate([pair_slot[half:], pair_slot[:half]])
        slots = jnp.arange(2 * classes, dtype=jnp.int32)
        has_pair = slots[:, None] == jnp.where(pair_slot >= 0, pair_slot, -1)[None, :]
        partner = jnp.max(jnp.where(has_pair, other_slot[None, :], -1), axis=1)
        mates = dot((partner[:, None] == slots[None, :]).astype(jnp.bfloat16), sent).astype(jnp.bfloat16)
        left = jnp.concatenate([sent, swapped(sent, "core", 1)], axis=0)
        right = jnp.concatenate([mates, swapped(mates, "core", 1)], axis=0)
        block_rows, block_cols = width // row_count, width // group_count
        picked = jnp.arange(width // 2, dtype=jnp.int32)
        picked = (picked // block_rows * 2 + core) * block_rows + picked % block_rows
        columns = jnp.arange(width, dtype=jnp.int32)
        pick = (picked[:, None] == columns[None, :]).astype(jnp.bfloat16)
        left = lax.dot_general(
            left, pick, (((1,), (1,)), ((), ())), preferred_element_type=jnp.float32
        ).astype(jnp.bfloat16)
        worker_terms = gram(left, right)

        came, worker_terms, pick = lax.optimization_barrier((came, worker_terms, pick))
        firm_pair = firm_halves(came, firms_here, width)
        terms = all_terms(
            firm_pair, swapped(firm_pair, "core", 1), pick, worker_terms, x_count, group_count
        )
        terms = terms.reshape(x_count * group_count, -1, block_cols)
        terms = lax.all_to_all(terms, ("x", "group"), 0, 0, tiled=True)
        wide = [terms[i].astype(jnp.float32) for i in range(x_count * group_count)]
        terms = sum(wide[1:], wide[0])
        terms = lax.all_to_all(
            terms.reshape(z_count, block_rows, block_cols), "z", 0, 0, tiled=True
        )
        total = sum([terms[i] for i in range(1, z_count)], terms[0])
        return total * (1.0 / (classes * local_rows))

    placed = (P(EVERYONE, None), P(EVERYONE), P(EVERYONE))
    return jax.shard_map(
        local, mesh=fine, in_specs=placed, out_specs=P(("x", "z", "core"), "group"), check_vma=False
    )
```

```python
import jax
import jax.numpy as jnp
from jax import lax
from jax.experimental import pallas as pl
from jax.experimental.pallas import tpu as pltpu
from jax.sharding import Mesh, PartitionSpec as P

LANES = 128
AXES = ("x", "z", "core", "group")
EVERYONE = AXES
FIRMS = 32768
WORKERS = 65536


def equal_before(keys):
    index = jnp.arange(keys.shape[0], dtype=jnp.int32)
    same = (keys[:, None] == keys[None, :]) & (index[:, None] < index[None, :])
    return jnp.sum(same.astype(jnp.int32), axis=0)


def one_hot(targets, number):
    rows = lax.broadcasted_iota(jnp.int32, (number, targets.shape[0]), 0)
    return (rows == targets[None, :]).astype(jnp.bfloat16)


def placed_values(targets, values, number):
    rows = lax.broadcasted_iota(jnp.int32, (number, targets.shape[0]), 0)
    return jnp.max(jnp.where(rows == targets[None, :], values[None, :], -1), axis=1)


def dot(a, b):
    return jnp.dot(a, b, preferred_element_type=jnp.float32)


def gram(a, b):
    return lax.dot_general(a, b, (((0,), (0,)), ((), ())), preferred_element_type=jnp.float32)


def swapped(value, axis, bit):
    size = lax.axis_size(axis)
    return lax.ppermute(value, axis, [(i, i ^ bit) for i in range(size)])


def swap_bits(held, before):
    shape = held.shape
    for axis in ("x", "core", "group"):
        bit = lax.axis_size(axis) // 2
        while bit:
            view = held.reshape(before, 2, -1)
            high = (lax.axis_index(axis) & bit) > 0
            keep = jnp.where(high, view[:, 1], view[:, 0])
            send = jnp.where(high, view[:, 0], view[:, 1])
            came = swapped(send, axis, bit)
            low_part = jnp.where(high, came, keep)
            high_part = jnp.where(high, keep, came)
            held = jnp.stack([low_part, high_part], axis=1)
            before *= 2
            bit //= 2
    return held.reshape(shape)


def pack_rows(targets, rows, slots):
    count, width = rows.shape
    step = 512

    def kernel(targets_ref, rows_ref, out_ref):
        first = pl.program_id(0) * step
        names = lax.broadcasted_iota(jnp.int32, (step, count), 0) + first
        hits = (names == targets_ref[...]).astype(jnp.float32).astype(jnp.bfloat16)
        out_ref[...] = dot(hits, rows_ref[...]).astype(jnp.bfloat16)

    return pl.pallas_call(
        kernel,
        grid=(slots // step,),
        in_specs=[
            pl.BlockSpec((1, count), lambda i: (0, 0)),
            pl.BlockSpec((count, width), lambda i: (0, 0)),
        ],
        out_specs=pl.BlockSpec((step, width), lambda i: (i, 0)),
        out_shape=jax.ShapeDtypeStruct((slots, width), jnp.bfloat16),
        compiler_params=pltpu.CompilerParams(vmem_limit_bytes=60 * 1024 * 1024),
        cost_estimate=pl.CostEstimate(
            flops=2 * slots * count * width, bytes_accessed=6 * 1024 * 1024, transcendentals=0
        ),
    )(targets[None, :], rows)


def slot_sums(slots_of, rows, tail):
    count, width = rows.shape
    slots, lanes = tail.shape
    step = 512

    def kernel(slots_ref, rows_ref, tail_ref, out_ref, hits_ref):
        j = pl.program_id(0)

        @pl.when(j == 0)
        def _():
            names = lax.broadcasted_iota(jnp.int32, (slots, step), 0)
            for at in range(0, count, step):
                hits = names == slots_ref[:, at : at + step]
                hits_ref[:, at : at + step] = hits.astype(jnp.float32).astype(jnp.bfloat16)
            out_ref[:, width:] = tail_ref[...]

        here = pl.ds(pl.multiple_of(j * step, step), step)
        out_ref[:, here] = dot(hits_ref[...], rows_ref[...]).astype(jnp.bfloat16)

    return pl.pallas_call(
        kernel,
        grid=(width // step,),
        in_specs=[
            pl.BlockSpec((1, count), lambda j: (0, 0)),
            pl.BlockSpec((count, step), lambda j: (0, j)),
            pl.BlockSpec((slots, lanes), lambda j: (0, 0)),
        ],
        out_specs=pl.BlockSpec((slots, width + lanes), lambda j: (0, 0)),
        out_shape=jax.ShapeDtypeStruct((slots, width + lanes), jnp.bfloat16),
        scratch_shapes=[pltpu.VMEM((slots, count), jnp.bfloat16)],
        compiler_params=pltpu.CompilerParams(vmem_limit_bytes=16 * 1024 * 1024),
        cost_estimate=pl.CostEstimate(
            flops=2 * slots * count * width, bytes_accessed=6 * 1024 * 1024, transcendentals=0
        ),
    )(slots_of[None, :], rows, tail)


def firm_halves(came, firms, width):
    count, lanes = came.shape[0], came.shape[1] - width

    def kernel(came_ref, out_ref):
        names = lax.broadcasted_iota(jnp.int32, (count, lanes), 1).astype(jnp.float32)
        hits = (came_ref[:, width:].astype(jnp.float32) == names).astype(jnp.float32).astype(jnp.bfloat16)
        sums = gram(hits, came_ref[:, :width])
        high = sums.astype(jnp.bfloat16)
        out_ref[:firms] = high
        out_ref[firms:] = (sums - high.astype(jnp.float32)).astype(jnp.bfloat16)

    return pl.pallas_call(
        kernel,
        out_shape=jax.ShapeDtypeStruct((2 * firms, width), jnp.bfloat16),
        compiler_params=pltpu.CompilerParams(vmem_limit_bytes=12 * 1024 * 1024),
        cost_estimate=pl.CostEstimate(
            flops=2 * count * firms * width, bytes_accessed=2 * 1024 * 1024, transcendentals=0
        ),
    )(came)


def all_terms(own, other, pick, worker_terms, row_parts, col_parts):
    firms, width = own.shape[0] // 2, own.shape[1]
    picked = pick.shape[0]
    cols = width // col_parts

    def kernel(own_ref, other_ref, pick_ref, terms_ref, out_ref, high_ref, low_ref, left_ref):
        g = pl.program_id(0)

        @pl.when(g == 0)
        def _():
            high_ref[:firms] = own_ref[:firms]
            high_ref[firms:] = other_ref[:firms]
            low_ref[:firms] = own_ref[firms:]
            low_ref[firms:] = other_ref[firms:]
            across = (((1,), (1,)), ((), ()))
            for at, ref in ((0, high_ref), (2 * firms, low_ref)):
                left_ref[:, at : at + 2 * firms] = lax.dot_general(
                    pick_ref[...], ref[...], across, preferred_element_type=jnp.float32
                ).astype(jnp.bfloat16)

        here = pl.ds(pl.multiple_of(g * cols, cols), cols)
        high, low = high_ref[:, here], low_ref[:, here]
        left_high, left_low = left_ref[:, : 2 * firms], left_ref[:, 2 * firms :]
        sums = terms_ref[...] + (dot(left_high, low) + dot(left_low, high)) + dot(left_high, high)
        out_ref[...] = sums.astype(jnp.bfloat16).reshape(out_ref.shape)

    return pl.pallas_call(
        kernel,
        grid=(col_parts,),
        in_specs=[
            pl.BlockSpec((2 * firms, width), lambda g: (0, 0)),
            pl.BlockSpec((2 * firms, width), lambda g: (0, 0)),
            pl.BlockSpec((picked, width), lambda g: (0, 0)),
            pl.BlockSpec((picked, cols), lambda g: (0, g)),
        ],
        out_specs=pl.BlockSpec((row_parts, 1, picked // row_parts, cols), lambda g: (0, g, 0, 0)),
        out_shape=jax.ShapeDtypeStruct((row_parts, col_parts, picked // row_parts, cols), jnp.bfloat16),
        scratch_shapes=[
            pltpu.VMEM((2 * firms, width), jnp.bfloat16),
            pltpu.VMEM((2 * firms, width), jnp.bfloat16),
            pltpu.VMEM((picked, 4 * firms), jnp.bfloat16),
        ],
        compiler_params=pltpu.CompilerParams(vmem_limit_bytes=52 * 1024 * 1024),
        cost_estimate=pl.CostEstimate(
            flops=2 * picked * width * 10 * firms, bytes_accessed=6 * 1024 * 1024, transcendentals=0
        ),
    )(own, other, pick, worker_terms)


def solution(mesh):
    row_count, group_count = mesh.shape["rows"], mesh.shape["group"]
    classes = row_count * group_count
    x_count, z_count = 4, row_count // 8
    fine = Mesh(mesh.devices.reshape(x_count, z_count, 2, group_count), AXES)
    workers_here = WORKERS // classes
    firms_here = FIRMS // classes

    def local(scores, worker_ids, firm_ids):
        local_rows, width = scores.shape
        capacity = 2 * local_rows // classes
        core = lax.axis_index("core")

        raw = jnp.broadcast_to((worker_ids * FIRMS + firm_ids)[None, :], (z_count, local_rows))
        raw, worker_ids = lax.optimization_barrier((raw, worker_ids))
        raw = lax.all_to_all(raw, "z", 0, 0, tiled=True)

        home = worker_ids % classes
        target = home * capacity + equal_before(home)
        packed = pack_rows(target, scores, classes * capacity)
        packed, raw = lax.optimization_barrier((packed, raw))
        got = lax.all_to_all(packed, EVERYONE, 0, 0, tiled=True)

        inner = 2 * group_count
        raw_worker = raw // FIRMS
        raw_home = raw_worker % classes
        mine = (raw_home // inner) % z_count == lax.axis_index("z")
        across = (raw_home // (inner * z_count)) * inner + raw_home % inner
        across = jnp.where(mine, across, -1)
        slot = jnp.where(mine, across * capacity + jax.vmap(equal_before)(across), -1)
        raw_code = (raw_worker // classes) * FIRMS + raw % FIRMS
        slot_codes = jax.vmap(lambda t, v: placed_values(t, v, x_count * inner * capacity))(slot, raw_code)
        codes = swap_bits(slot_codes, z_count)
        codes = codes.reshape(z_count, x_count, -1).transpose(1, 0, 2).reshape(-1)

        used = codes >= 0
        worker = jnp.where(used, codes // FIRMS, -1)
        firm = jnp.where(used, codes % FIRMS, -1)
        table = lax.broadcasted_iota(jnp.int32, (workers_here, codes.shape[0]), 0) == worker[None, :]
        first = jnp.min(jnp.where(table, firm[None, :], 2**30), axis=1)
        row_first = jnp.max(jnp.where(table, first[:, None], -1), axis=0)
        pair = jnp.where(used, worker + workers_here * (firm != row_first).astype(jnp.int32), -1)
        pair_firm = placed_values(pair, firm, 2 * workers_here)
        firm_home = jnp.where(pair_firm >= 0, pair_firm % classes, -1)
        pair_slot = jnp.where(pair_firm >= 0, 2 * firm_home + equal_before(firm_home), -1)
        pair_rows = lax.broadcasted_iota(jnp.int32, (2 * workers_here, codes.shape[0]), 0)
        row_slot = jnp.max(jnp.where(pair_rows == pair[None, :], pair_slot[:, None], -1), axis=0)
        sent_firm = placed_values(pair_slot, pair_firm // classes, 2 * classes)

        tail = jnp.broadcast_to(sent_firm.astype(jnp.bfloat16)[:, None], (2 * classes, LANES))
        tail, row_slot, got = lax.optimization_barrier((tail, row_slot, got))
        sent = slot_sums(row_slot, got, tail)
        came = lax.all_to_all(sent, EVERYONE, 0, 0, tiled=True)
        sent = sent[:, :width]

        half = workers_here
        other_slot = jnp.concatenate([pair_slot[half:], pair_slot[:half]])
        slots = jnp.arange(2 * classes, dtype=jnp.int32)
        has_pair = slots[:, None] == jnp.where(pair_slot >= 0, pair_slot, -1)[None, :]
        partner = jnp.max(jnp.where(has_pair, other_slot[None, :], -1), axis=1)
        mates = dot((partner[:, None] == slots[None, :]).astype(jnp.bfloat16), sent).astype(jnp.bfloat16)
        left = jnp.concatenate([sent, swapped(sent, "core", 1)], axis=0)
        right = jnp.concatenate([mates, swapped(mates, "core", 1)], axis=0)
        block_rows, block_cols = width // row_count, width // group_count
        picked = jnp.arange(width // 2, dtype=jnp.int32)
        picked = (picked // block_rows * 2 + core) * block_rows + picked % block_rows
        columns = jnp.arange(width, dtype=jnp.int32)
        pick = (picked[:, None] == columns[None, :]).astype(jnp.bfloat16)
        left = lax.dot_general(
            left, pick, (((1,), (1,)), ((), ())), preferred_element_type=jnp.float32
        ).astype(jnp.bfloat16)
        worker_terms = gram(left, right)

        came, worker_terms, pick = lax.optimization_barrier((came, worker_terms, pick))
        firm_pair = firm_halves(came, firms_here, width)
        terms = all_terms(
            firm_pair, swapped(firm_pair, "core", 1), pick, worker_terms, x_count, group_count
        )
        terms = terms.reshape(x_count * group_count, -1, block_cols)
        terms = lax.all_to_all(terms, ("x", "group"), 0, 0, tiled=True)
        wide = [terms[i].astype(jnp.float32) for i in range(x_count * group_count)]
        terms = sum(wide[1:], wide[0])
        terms = lax.all_to_all(
            terms.reshape(z_count, block_rows, block_cols), "z", 0, 0, tiled=True
        )
        total = sum([terms[i] for i in range(1, z_count)], terms[0])
        return total * (1.0 / (classes * local_rows))

    placed = (P(EVERYONE, None), P(EVERYONE), P(EVERYONE))
    return jax.shard_map(
        local, mesh=fine, in_specs=placed, out_specs=P(("x", "z", "core"), "group"), check_vma=False
    )
```
